32 devices in a mesh: parts: 1, axial: 8 (over y, x, core), radial: 4 (over z).
Axes of the slice: x: 2, y: 2, z: 4, core: 2. Of those that a mesh axis runs over, the one named last changes fastest.
Arguments:
- inputs: bfloat16 [64, 64, 8192], P(None, 'radial', ('parts', 'axial')), may hold values from -6 to 6
- saved_pre: bfloat16 [64, 64, 8192], P(None, 'radial', ('parts', 'axial')), may hold values from -6 to 6
- cotangent: bfloat16 [64, 64, 8192], P(None, 'radial', ('parts', 'axial')), may hold values from -24 to 24
- pointwise_weight: bfloat16 [64, 64], replicated, may hold values from -0.75 to 0.75
- spectral_weight: bfloat16 [32, 256, 64, 128], P('radial', 'axial'), may hold values from -3 to 3
Outputs:
- input_grad: bfloat16 [64, 64, 8192], P(None, 'radial', ('parts', 'axial'))
- spectral_grad: float32 [32, 256, 64, 128], P('radial', ('parts', 'axial'))
- weight_grad: float32 [64, 64], P('parts')
The draws below stay inside these ranges and needn't reach their ends.
All inputs are finite; a program needn't handle non-finite values.
Results may differ from the reference program's by a relative error of at most 0.0053.
Values may be sent and summed in bfloat16 or wider, within the bound.
A program may use at most 128 MiB of HBM per device.

```python
import math
import jax
import jax.numpy as jnp
from jax import lax

C = 64
KA = 256
KR = 32
AX_DEV = 1024
RADIAL = 64
AXIAL = 8192
N_AXIAL = 8


def draw_cotangent(key, part):
    axial_ramp = 1.0 + 2.0 * jnp.arange(AXIAL, dtype=jnp.float32) / max(AXIAL - 1, 1)
    radial_ramp = 1.0 + jnp.arange(RADIAL, dtype=jnp.float32) / max(RADIAL - 1, 1)
    envelope = radial_ramp[None, :, None] * axial_ramp[None, None, :]
    base = jnp.clip(jax.random.normal(key, (C, RADIAL, AXIAL), jnp.float32), -4.0, 4.0)
    return (base * envelope).astype(jnp.bfloat16)


def steps_of(own_key, shape, pieces, least, high):
    factor_of, own = 1.0, jax.random.fold_in(own_key, 6)
    for axis_at, parts in pieces:
        draws = jnp.exp(jax.random.uniform(jax.random.fold_in(own, axis_at), (parts,), jnp.float32, least / len(pieces), high / len(pieces)))
        factor_of = factor_of * jnp.repeat(draws, shape[axis_at] // parts).reshape([-1 if axis == axis_at else 1 for axis in range(len(shape))])
    return factor_of


def centred(rng, shape, scale, bound, cuts=(), kind=jnp.bfloat16):
    array = scale * jax.random.normal(rng, shape, jnp.float32)
    if cuts:
        array = array * steps_of(rng, shape, cuts, -0.22, 0.18)
    return jnp.clip(array, -bound, bound).astype(kind)


def setup_inputs(seed: int = 0, part: int = 0) -> dict:
    splits = jax.random.split(jax.random.key(seed), 6)
    part_keys = jax.random.split(jax.random.fold_in(splits[5], part), 6)
    inputs = centred(part_keys[0], (C, RADIAL, AXIAL), 1.0, 6.0, ((1, 4), (2, 8)))
    saved_pre = centred(part_keys[1], (C, RADIAL, AXIAL), 1.0, 6.0, ((1, 4), (2, 8)))
    cotangent = draw_cotangent(jax.random.fold_in(jax.random.fold_in(splits[5], part), 71), part)
    pointwise_weight = centred(splits[3], (C, C), C ** -0.5, 0.75)
    spectral_weight = centred(splits[4], (KR, KA, C, 2 * C), 0.5, 3.0, ((0, 4), (1, 8)))
    return {"inputs": inputs, "saved_pre": saved_pre, "cotangent": cotangent, "pointwise_weight": pointwise_weight, "spectral_weight": spectral_weight}


def axial_table(first, count, modes, total):
    points = first + jnp.arange(count, dtype=jnp.int32)
    orders = jnp.arange(modes, dtype=jnp.int32)
    phase = (points[:, None] * orders[None, :] % total).astype(jnp.float32) * (2.0 * math.pi / total)
    return jnp.stack([jnp.cos(phase), -jnp.sin(phase)], axis=2).reshape(count, 2 * modes).astype(jnp.bfloat16)

def radial_table(first, count, rows_first, rows_count, kept, total):
    orders = first + jnp.arange(count, dtype=jnp.int32)
    freqs = orders + jnp.where(orders >= kept // 2, total - kept, 0).astype(jnp.int32)
    rows = rows_first + jnp.arange(rows_count, dtype=jnp.int32)
    phase = (freqs[:, None] * rows[None, :] % total).astype(jnp.float32) * (2.0 * math.pi / total)
    return (jnp.cos(phase), jnp.sin(phase))

def gelu_slope(pre):
    value = pre.astype(jnp.float32)
    return 0.5 * (1.0 + jax.scipy.special.erf(value / math.sqrt(2.0))) + value * jnp.exp(-0.5 * value * value) / math.sqrt(2.0 * math.pi)

def spectrum(field):

    def step_fn(total, block):
        start = (block * AX_DEV).astype(jnp.int32)
        segment = lax.dynamic_slice_in_dim(field, start, AX_DEV, 2).astype(jnp.float32)
        table = axial_table(start, AX_DEV, KA, AXIAL).astype(jnp.float32)
        part = jnp.einsum('cra,aj->jcr', segment, table, precision=lax.Precision.HIGHEST)
        return (total + part, None)
    start_sum = jnp.zeros((2 * KA, C, RADIAL), jnp.float32)
    total, unused = lax.scan(step_fn, start_sum, jnp.arange(N_AXIAL, dtype=jnp.int32))
    return total

def to_modes(axial_part, cos_r, sin_r):
    split = axial_part.reshape(KA, 2, C, RADIAL)
    real_in = split[:, 0]
    imag_in = split[:, 1]
    high = lax.Precision.HIGHEST
    real_out = jnp.einsum('qr,kcr->qkc', cos_r, real_in, precision=high) + jnp.einsum('qr,kcr->qkc', sin_r, imag_in, precision=high)
    imag_out = jnp.einsum('qr,kcr->qkc', cos_r, imag_in, precision=high) - jnp.einsum('qr,kcr->qkc', sin_r, real_in, precision=high)
    return (real_out, imag_out)

def reference(inputs, saved_pre, cotangent, pointwise_weight, spectral_weight):
    high = lax.Precision.HIGHEST
    grad_pre = (cotangent.astype(jnp.float32) * gelu_slope(saved_pre)).astype(jnp.bfloat16)
    cos_r, sin_r = radial_table(0, KR, 0, RADIAL, KR, RADIAL)
    x_real, x_imag = to_modes(spectrum(inputs), cos_r, sin_r)
    g_real, g_imag = to_modes(spectrum(grad_pre), cos_r, sin_r)
    orders = jnp.arange(KA, dtype=jnp.int32)
    scales = jnp.where(orders == 0, 1.0, 2.0).astype(jnp.float32) / (RADIAL * AXIAL)
    dy_real = g_real * scales[None, :, None]
    dy_imag = g_imag * scales[None, :, None]
    grad_real = x_real[..., :, None] * dy_real[..., None, :] + x_imag[..., :, None] * dy_imag[..., None, :]
    grad_imag = x_real[..., :, None] * dy_imag[..., None, :] - x_imag[..., :, None] * dy_real[..., None, :]
    spectral_grad = jnp.concatenate([grad_real, grad_imag], axis=3)
    w_real = spectral_weight[..., :C].astype(jnp.float32)
    w_imag = spectral_weight[..., C:].astype(jnp.float32)
    dx_real = jnp.einsum('qkio,qko->qki', w_real, dy_real, precision=high) + jnp.einsum('qkio,qko->qki', w_imag, dy_imag, precision=high)
    dx_imag = jnp.einsum('qkio,qko->qki', w_real, dy_imag, precision=high) - jnp.einsum('qkio,qko->qki', w_imag, dy_real, precision=high)
    back_real = jnp.einsum('qr,qkc->kcr', cos_r, dx_real, precision=high) - jnp.einsum('qr,qkc->kcr', sin_r, dx_imag, precision=high)
    back_imag = jnp.einsum('qr,qkc->kcr', sin_r, dx_real, precision=high) + jnp.einsum('qr,qkc->kcr', cos_r, dx_imag, precision=high)
    back = jnp.stack([back_real, back_imag], axis=1).astype(jnp.bfloat16).reshape(2 * KA, C, RADIAL)
    table = axial_table(0, AXIAL, KA, AXIAL).astype(jnp.float32)
    spectral_part = jnp.einsum('jcr,aj->cra', back.astype(jnp.float32), table, precision=high)
    flat_grad = grad_pre.astype(jnp.float32).reshape(C, RADIAL * AXIAL)
    flat_in = inputs.astype(jnp.float32).reshape(C, RADIAL * AXIAL)
    point_part = jnp.dot(pointwise_weight.astype(jnp.float32), flat_grad, precision=high)
    input_grad = (point_part + spectral_part.reshape(C, RADIAL * AXIAL)).astype(jnp.bfloat16).reshape(C, RADIAL, AXIAL)
    weight_grad = jnp.dot(flat_in, flat_grad.T, precision=high) / math.sqrt(RADIAL * AXIAL)
    return (input_grad, spectral_grad, weight_grad)
```

```python
import functools
import math

import jax
import jax.numpy as jnp
import numpy as np
from jax import lax
from jax.experimental import pallas as pl
from jax.experimental.pallas import tpu as pltpu
from jax.sharding import PartitionSpec as P

KA = 256
KR = 32
LANES = 128
BF = jnp.bfloat16
F32 = jnp.float32
VMEM_LIMIT = 56 * 1024 * 1024


def axial_factors(n_axial, ax_cols):
    total = n_axial * ax_cols
    own = KA // n_axial
    col = np.arange(2 * KA)
    mode = (col // (2 * own)) * own + col % own
    turn = (col // own) % 2
    points = np.arange(LANES)
    low = (points[:, None] * mode[None, :] % total) * (2.0 * np.pi / total)
    starts = np.arange(total // LANES) * LANES
    high = (starts[:, None] * mode[None, :] % total) * (2.0 * np.pi / total)
    high = high + turn[None, :] * (np.pi / 2)
    as32 = lambda value: value.astype(np.float32)
    return as32(np.cos(low)), as32(np.sin(low)), as32(np.cos(high)), as32(np.sin(high))


def split16(value):
    high = value.astype(BF)
    return high, (value - high.astype(F32)).astype(BF)


def gelu_slope(value):
    return 0.5 * (1.0 + lax.erf(value * (1.0 / math.sqrt(2.0)))) + value * jnp.exp(
        -0.5 * value * value
    ) * (1.0 / math.sqrt(2.0 * math.pi))


def local_kernel(
    n_axial, x_ref, s_ref, c_ref, cl_ref, sl_ref, ch_ref, sh_ref, px_ref, pg_ref, grad_ref, table
):
    _, some, rad_rows, cols = x_ref.shape
    lines = some * rad_rows
    half = 2 * KA // n_axial
    pieces = cols // LANES

    @pl.when(pl.program_id(0) == 0)
    def _():
        first = lax.axis_index("axial") * pieces
        for u in range(pieces):
            at = pl.ds(first + u, 1)
            table[u * LANES : (u + 1) * LANES, :] = (
                ch_ref[at, :] * cl_ref[...] - sh_ref[at, :] * sl_ref[...]
            ).astype(BF)

    def spread(value, out_ref):
        for d in range(n_axial):
            lanes = slice(d * half, (d + 1) * half)
            out_ref[d] = jnp.concatenate([value[:lines, lanes], value[lines:, lanes]], axis=1).astype(BF)

    waves = table[...]
    spread(
        jnp.dot(x_ref[...].reshape(2 * lines, cols), waves, preferred_element_type=F32), px_ref
    )
    for h in range(2):
        for c in range(some):
            slope = gelu_slope(s_ref[h, c].astype(F32))
            grad_ref[h, c] = (c_ref[h, c].astype(F32) * slope).astype(BF)
    spread(
        jnp.dot(grad_ref[...].reshape(2 * lines, cols), waves, preferred_element_type=F32), pg_ref
    )


def radial_matrices(n_radial, rad_rows, rad, group):
    total = n_radial * rad_rows
    shape = (KR * group, group * rad_rows)
    row = lax.broadcasted_iota(jnp.int32, shape, 0)
    col = lax.broadcasted_iota(jnp.int32, shape, 1)
    q = row // group
    freq = q + jnp.where(q >= KR // 2, total - KR, 0)
    point = rad * rad_rows + col % rad_rows
    phase = (freq * point % total).astype(F32) * (2.0 * math.pi / total)
    same = row % group == col // rad_rows
    return jnp.where(same, jnp.cos(phase), 0.0), jnp.where(same, jnp.sin(phase), 0.0)


def comm_kernel(
    n_axial, n_radial, final_scale,
    px_ref, pg_ref, w_hbm, x_hbm, g_hbm, scale_ref,
    spec_ref, gath_ref, wg_ref,
    w_vmem, x_vmem, g_vmem, pair_in, q_buf, chip_in, r_buf, r16, rad_in, dx_all, dx32,
    wl_own, wl_pair, wl_chip, wl_rad, fwd, bwd,
    in_sem, ps, pr, cs, cr, rs, rr, ds_, dr, as_, ar, fs, fr, wps, wpr, wcs, wcr, wrs, wrr,
):
    chips = n_axial // 2
    ax = lax.axis_index("axial")
    rad = lax.axis_index("radial")
    chip = ax // 2
    core = ax % 2
    partner = chip * 2 + 1 - core
    own_k = KA // n_axial
    half = 2 * own_k
    q_own, channels, lanes = spec_ref.shape
    cut = channels // 2
    rad_rows = x_vmem.shape[1]
    cols = x_vmem.shape[2]
    lines = channels * rad_rows
    group = 8
    rows = group * rad_rows
    parts = (pg_ref, px_ref)

    def remote(src, dst, send, recv, where):
        return pltpu.make_async_remote_copy(
            src_ref=src, dst_ref=dst, send_sem=send, recv_sem=recv,
            device_id=where, device_id_type=pl.DeviceIdType.MESH,
        )

    local = [
        pltpu.make_async_copy(x_hbm, x_vmem, in_sem.at[0]),
        pltpu.make_async_copy(g_hbm, g_vmem, in_sem.at[1]),
        pltpu.make_async_copy(w_hbm, w_vmem, in_sem.at[2]),
    ]
    peers = [(chip + t) % chips for t in range(chips)]
    rads = [(rad + t) % n_radial for t in range(n_radial)]
    barrier = pltpu.get_barrier_semaphore()
    greet = [{"axial": partner}]
    greet += [{"axial": peers[t] * 2 + core} for t in range(1, chips)]
    greet += [{"radial": rads[t]} for t in range(1, n_radial)]
    for where in greet:
        pl.semaphore_signal(barrier, inc=1, device_id=where, device_id_type=pl.DeviceIdType.MESH)
    pl.semaphore_wait(barrier, len(greet))

    sent = []
    order = list(range(1, chips)) + [0]
    pair = {}
    for f in range(2):
        for t in order:
            pair[f, t] = remote(
                parts[f].at[peers[t] * 2 + 1 - core], pair_in.at[f, t], ps.at[f, t], pr.at[f, t],
                {"axial": partner},
            )
            pair[f, t].start()
    sent += list(pair.values())
    for copy in local:
        copy.start()
    chip_copies = {}
    for f in range(2):
        for t in order[:-1]:
            pair[f, t].wait_recv()
            q_buf[f, t - 1] = (
                parts[f][peers[t] * 2 + core].astype(F32) + pair_in[f, t].astype(F32)
            ).astype(BF)
            chip_copies[f, t] = remote(
                q_buf.at[f, t - 1], chip_in.at[f, t - 1], cs.at[f, t - 1], cr.at[f, t - 1],
                {"axial": peers[t] * 2 + core},
            )
            chip_copies[f, t].start()
        pair[f, 0].wait_recv()
    sent += list(chip_copies.values())

    cos_m, sin_m = radial_matrices(n_radial, rad_rows, rad, group)
    both = jnp.concatenate([cos_m, sin_m], axis=1)
    high, low = split16(both)
    fwd[...] = jnp.concatenate([high, high, low], axis=1)
    both = jnp.concatenate([cos_m.T, sin_m.T], axis=1)
    high, low = split16(both)
    bwd[...] = jnp.concatenate([high, low], axis=1)

    def transform(f):
        for t in range(1, chips):
            chip_copies[f, t].wait_recv()
        forward = fwd[...]

        for i in range(cut // group):
            at = pl.ds(i * rows, rows)
            z = parts[f][ax, at, :].astype(F32) + pair_in[f, 0, at, :].astype(F32)
            for t in range(chips - 1):
                z = z + chip_in[f, t, at, :].astype(F32)
            turned = jnp.concatenate(
                [z[:, own_k:half], -z[:, :own_k], z[:, half + own_k :], -z[:, half : half + own_k]],
                axis=1,
            )
            zh, zl = split16(z)
            th, tl = split16(turned)
            stack = jnp.concatenate([zh, th, zl, tl, zh, th], axis=0)
            out = jnp.dot(forward, stack, preferred_element_type=F32)
            r_buf[f, :, i * group : (i + 1) * group, :] = out.reshape(KR, group, lanes)
        copies = []
        for t in range(1, n_radial):
            r16[f, t - 1] = r_buf[f, pl.ds(rads[t] * q_own, q_own)].astype(BF)
            copy = remote(
                r16.at[f, t - 1], rad_in.at[f, t - 1], rs.at[f, t - 1], rr.at[f, t - 1],
                {"radial": rads[t]},
            )
            copy.start()
            copies.append(copy)
        return copies

    def collect(f, q):
        value = r_buf[f, rad * q_own + q]
        for t in range(n_radial - 1):
            value = value + rad_in[f, t, q].astype(F32)
        return jnp.concatenate([value[:, :half], value[:, half:]], axis=0)

    rad_g = transform(0)

    local[0].wait()
    local[1].wait()
    piece = 256
    per = piece // rad_rows
    grads = g_vmem[...].reshape(lines, cols)

    def gram(i, carry):
        block = x_vmem[pl.ds(i * per, per)].reshape(piece, cols)
        full = lax.dot_general(block, grads, (((1,), (1,)), ((), ())), preferred_element_type=F32)
        full = full.reshape(per, rad_rows, lines)
        row = lax.broadcasted_iota(jnp.int32, full.shape, 1)
        col = lax.broadcasted_iota(jnp.int32, full.shape, 2) % rad_rows
        picked = jnp.sum(jnp.where(row == col, full, 0.0), axis=1)
        line = lax.broadcasted_iota(jnp.int32, (lines, channels), 0) // rad_rows
        chan = lax.broadcasted_iota(jnp.int32, (lines, channels), 1)
        chooser = jnp.where(line == chan, 1.0, 0.0).astype(F32)
        wl_own[pl.ds(pl.multiple_of(i * per, per), per), :] = jnp.dot(
            picked, chooser, preferred_element_type=F32, precision=lax.Precision.HIGHEST
        )
        return carry

    lax.fori_loop(0, lines // piece, gram, 0)
    wl_first = remote(wl_own, wl_pair, wps, wpr, {"axial": partner})
    wl_first.start()

    rad_x = transform(1)
    sent += rad_g + rad_x + [wl_first]
    wl_first.wait_recv()
    wl_chip[chip] = wl_own[...] + wl_pair[...]
    wl_copies = []
    for t in range(1, chips):
        copy = remote(
            wl_chip.at[chip], wl_chip.at[chip], wcs.at[t - 1], wcr.at[t - 1],
            {"axial": peers[t] * 2 + core},
        )
        copy.start()
        wl_copies.append(copy)
    sent += wl_copies

    local[2].wait()
    for copy in rad_g:
        copy.wait_recv()

    def modes(q, carry):
        g = collect(0, q) * scale_ref[...]
        spec_ref[q, :, half:] = g
        turned = jnp.concatenate([g[:, own_k:], -g[:, :own_k]], axis=1)
        gh, gl = split16(g)
        th, tl = split16(turned)
        side = jnp.concatenate(
            [jnp.concatenate([gh, gl], axis=1), jnp.concatenate([th, tl], axis=1)], axis=0
        )
        out = jnp.dot(
            w_vmem[q].reshape(own_k * channels, 2 * channels), side, preferred_element_type=F32
        )
        lane = lax.broadcasted_iota(jnp.int32, (channels, lanes), 1) % own_k
        total = jnp.zeros((channels, lanes), F32)
        for k in range(own_k):
            total = jnp.where(lane == k, out[k * channels : (k + 1) * channels], total)
        dx = total[:, :half] + total[:, half:]
        dx_all[rad, q] = jnp.concatenate([dx[:cut], dx[cut:]], axis=1).astype(BF)
        return carry

    lax.fori_loop(0, q_own, modes, 0)
    dx_copies = []
    for t in range(1, n_radial):
        copy = remote(dx_all.at[rad], dx_all.at[rad], ds_.at[t - 1], dr.at[t - 1], {"radial": rads[t]})
        copy.start()
        dx_copies.append(copy)
    sent += dx_copies

    for copy in wl_copies:
        copy.wait_recv()
    total = wl_chip[0]
    for t in range(1, chips):
        total = total + wl_chip[t]
    wl_rad[rad] = total
    wl_rad_copies = []
    for t in range(1, n_radial):
        copy = remote(
            wl_rad.at[rad], wl_rad.at[rad], wrs.at[t - 1], wrr.at[t - 1], {"radial": rads[t]}
        )
        copy.start()
        wl_rad_copies.append(copy)
    sent += wl_rad_copies

    for copy in dx_copies:
        copy.wait_recv()
    for t in range(n_radial):
        dx32[t * q_own : (t + 1) * q_own] = dx_all[t].astype(F32)
    backward = bwd[...]
    for i in range(cut // group):
        d = dx32[:, i * group : (i + 1) * group, :].reshape(KR * group, lanes)
        turned = jnp.concatenate(
            [-d[:, own_k:half], d[:, :own_k], -d[:, half + own_k :], d[:, half : half + own_k]], axis=1
        )
        d16 = d.astype(BF)
        t16 = turned.astype(BF)
        stack = jnp.concatenate([d16, t16, d16, t16], axis=0)
        gath_ref[ax, i * rows : (i + 1) * rows, :] = jnp.dot(
            backward, stack, preferred_element_type=F32
        ).astype(BF)
    gather = []
    for t in range(1, chips):
        copy = remote(
            gath_ref.at[ax], gath_ref.at[ax], as_.at[t - 1], ar.at[t - 1], {"axial": peers[t] * 2 + core}
        )
        copy.start()
        gather.append(copy)
    passed = [remote(gath_ref.at[ax], gath_ref.at[ax], fs.at[0], fr.at[0], {"axial": partner})]
    passed[0].start()

    for copy in rad_x:
        copy.wait_recv()

    def keep(q, carry):
        spec_ref[q, :, :half] = collect(1, q)
        return carry

    lax.fori_loop(0, q_own, keep, 0)
    for t in range(1, chips):
        gather[t - 1].wait_recv()
        slot = ((chip - t + chips) % chips) * 2 + core
        copy = remote(gath_ref.at[slot], gath_ref.at[slot], fs.at[t], fr.at[t], {"axial": partner})
        copy.start()
        passed.append(copy)

    for copy in wl_rad_copies:
        copy.wait_recv()
    total = wl_rad[0]
    for t in range(1, n_radial):
        total = total + wl_rad[t]
    wg_ref[...] = total * final_scale

    for copy in passed:
        copy.wait_recv()
    for copy in sent + gather + passed:
        copy.wait_send()


def outer_kernel(own_k, spec_ref, out_ref):
    half = 2 * own_k
    value = spec_ref[0]
    channels = value.shape[0]
    xh, xl = split16(value[:, :half])
    left = jnp.concatenate([xh, xl, xh], axis=1).reshape(channels // 16, 16, 3 * half)
    turned = jnp.transpose(value[:, half:])
    real, imag = turned[:own_k], turned[own_k:]
    sides = jnp.concatenate(
        [jnp.concatenate([real, imag], axis=1), jnp.concatenate([imag, -real], axis=1)], axis=0
    )
    sh, sl = split16(sides)
    right = jnp.concatenate([sh, sh, sl], axis=0)
    lane = lax.broadcasted_iota(jnp.int32, (16, 3 * half), 1) % own_k
    together = 8
    for first in range(0, own_k, together):
        rows = []
        for k in range(first, first + together):
            mask = jnp.where(lane == k, 1.0, 0.0).astype(BF)
            rows.append((left * mask[None]).reshape(channels, 3 * half))
        out = jnp.dot(jnp.concatenate(rows, axis=0), right, preferred_element_type=F32)
        out_ref[0, first : first + together] = out.reshape(together, channels, 2 * channels)


def final_kernel(
    n_axial, pw_ref, grad_ref, cl_ref, sl_ref, ch_ref, sh_ref, gath_ref, out_ref, left, table
):
    channels, rad_rows, cols = grad_ref.shape
    lines = channels * rad_rows
    half = 2 * KA // n_axial
    pieces = table.shape[1] // LANES
    step = pl.program_id(0)

    @pl.when(step == 0)
    def _():
        line = lax.broadcasted_iota(jnp.int32, (lines, channels), 0) // rad_rows
        chan = lax.broadcasted_iota(jnp.int32, (lines, channels), 1)
        chooser = jnp.where(line == chan, 1.0, 0.0).astype(BF)
        rows = jnp.dot(chooser, pw_ref[...], preferred_element_type=F32).astype(BF)
        dims = (((1,), (1,)), ((), ()))
        wide = lax.dot_general(rows, chooser, dims, preferred_element_type=F32)
        row = lax.broadcasted_iota(jnp.int32, wide.shape, 0) % rad_rows
        col = lax.broadcasted_iota(jnp.int32, wide.shape, 1) % rad_rows
        left[:, :lines] = jnp.where(row == col, wide, 0.0).astype(BF)
        cut = lines // 2
        for d in range(n_axial):
            lanes = slice(lines + d * half, lines + (d + 1) * half)
            left[:cut, lanes] = gath_ref[d, :, :half]
            left[cut:, lanes] = gath_ref[d, :, half:]
        first = pl.multiple_of(lax.axis_index("axial") * pieces, pieces)
        cos_high = jnp.transpose(ch_ref[pl.ds(first, pieces), :])
        sin_high = jnp.transpose(sh_ref[pl.ds(first, pieces), :])
        for u in range(pieces):
            table[:, u * LANES : (u + 1) * LANES] = (
                cos_high[:, u : u + 1] * cl_ref[...] - sin_high[:, u : u + 1] * sl_ref[...]
            ).astype(BF)

    waves = table[:, pl.ds(pl.multiple_of(step * cols, cols), cols)]
    right = jnp.concatenate([grad_ref[...].reshape(lines, cols), waves], axis=0)
    value = jnp.dot(left[...], right, preferred_element_type=F32)
    out_ref[...] = value.astype(BF).reshape(channels, rad_rows, cols)


def params(**more):
    return pltpu.CompilerParams(vmem_limit_bytes=VMEM_LIMIT, **more)


def body(inputs, saved_pre, cotangent, pointwise_weight, spectral_weight):
    channels, rad_rows, ax_cols = inputs.shape
    n_axial = lax.axis_size("axial")
    n_radial = lax.axis_size("radial")
    ax_index = lax.axis_index("axial")
    points = ax_cols * n_axial * rad_rows * n_radial
    own_k = KA // n_axial
    q_own = KR // n_radial
    lines = channels * rad_rows
    lanes = 4 * own_k
    chips = n_axial // 2
    cut = channels // 2

    cos_low, sin_low, cos_high, sin_high = axial_factors(n_axial, ax_cols)
    orders = ax_index * own_k + jnp.arange(own_k, dtype=jnp.int32)
    weights = jnp.where(orders == 0, 1.0, 2.0).astype(F32) / points
    scale = jnp.concatenate([weights, weights]).reshape(1, 2 * own_k)

    whole = lambda *shape: pl.BlockSpec(shape, lambda i: (0,) * len(shape))
    group = 8
    field = pl.BlockSpec((2, group, rad_rows, ax_cols), lambda i: (0, i, 0, 0))
    halves = lambda value: value.reshape(2, cut, rad_rows, ax_cols)
    part = pl.BlockSpec((n_axial, group * rad_rows, lanes), lambda i: (0, i, 0))
    part_shape = jax.ShapeDtypeStruct((n_axial, lines // 2, lanes), BF)
    part_x, part_g, grad_pre = pl.pallas_call(
        functools.partial(local_kernel, n_axial),
        grid=(cut // group,),
        in_specs=[
            field, field, field,
            whole(*cos_low.shape), whole(*cos_low.shape), whole(*cos_high.shape), whole(*cos_high.shape),
        ],
        out_specs=[part, part, field],
        out_shape=[
            part_shape,
            part_shape,
            jax.ShapeDtypeStruct((2, cut, rad_rows, ax_cols), BF),
        ],
        scratch_shapes=[pltpu.VMEM((ax_cols, 2 * KA), BF)],
        compiler_params=params(),
        name="local_transform",
    )(halves(inputs), halves(saved_pre), halves(cotangent), cos_low, sin_low, cos_high, sin_high)
    grad_pre = grad_pre.reshape(channels, rad_rows, ax_cols)

    vmem = pl.BlockSpec(memory_space=pltpu.VMEM)
    hbm = pl.BlockSpec(memory_space=pl.ANY)
    dma = lambda *count: pltpu.SemaphoreType.DMA(count)
    one = pltpu.SemaphoreType.DMA
    spec, gathered, weight_grad = pl.pallas_call(
        functools.partial(comm_kernel, n_axial, n_radial, 1.0 / math.sqrt(points)),
        in_specs=[vmem, vmem, hbm, hbm, hbm, vmem],
        out_specs=[vmem, vmem, vmem],
        out_shape=[
            jax.ShapeDtypeStruct((q_own, channels, lanes), F32),
            jax.ShapeDtypeStruct((n_axial, lines // 2, lanes), BF),
            jax.ShapeDtypeStruct((channels, channels), F32),
        ],
        scratch_shapes=[
            pltpu.VMEM(spectral_weight.shape, BF),
            pltpu.VMEM(inputs.shape, BF),
            pltpu.VMEM(inputs.shape, BF),
            pltpu.VMEM((2, chips, lines // 2, lanes), BF),
            pltpu.VMEM((2, chips - 1, lines // 2, lanes), BF),
            pltpu.VMEM((2, chips - 1, lines // 2, lanes), BF),
            pltpu.VMEM((2, KR, cut, lanes), F32),
            pltpu.VMEM((2, n_radial - 1, q_own, cut, lanes), BF),
            pltpu.VMEM((2, n_radial - 1, q_own, cut, lanes), BF),
            pltpu.VMEM((n_radial, q_own, cut, lanes), BF),
            pltpu.VMEM((KR, cut, lanes), F32),
            pltpu.VMEM((channels, channels), F32),
            pltpu.VMEM((channels, channels), F32),
            pltpu.VMEM((chips, channels, channels), F32),
            pltpu.VMEM((n_radial, channels, channels), F32),
            pltpu.VMEM((KR * group, 6 * group * rad_rows), BF),
            pltpu.VMEM((group * rad_rows, 4 * KR * group), BF),
            dma(3),
            dma(2, chips), dma(2, chips),
            dma(2, chips - 1), dma(2, chips - 1),
            dma(2, n_radial - 1), dma(2, n_radial - 1),
            dma(n_radial - 1), dma(n_radial - 1),
            dma(chips - 1), dma(chips - 1),
            dma(chips), dma(chips),
            one, one,
            dma(chips - 1), dma(chips - 1),
            dma(n_radial - 1), dma(n_radial - 1),
        ],
        compiler_params=params(collective_id=0, has_side_effects=True),
        name="exchange",
    )(part_x, part_g, spectral_weight, inputs, grad_pre, scale)

    spectral_grad = pl.pallas_call(
        functools.partial(outer_kernel, own_k),
        grid=(q_own,),
        in_specs=[pl.BlockSpec((1, channels, lanes), lambda i: (i, 0, 0))],
        out_specs=pl.BlockSpec((1, own_k, channels, 2 * channels), lambda i: (i, 0, 0, 0)),
        out_shape=jax.ShapeDtypeStruct((q_own, own_k, channels, 2 * channels), F32),
        compiler_params=params(),
        name="mode_products",
    )(spec)

    steps = 4
    cols = ax_cols // steps
    strip = pl.BlockSpec((channels, rad_rows, cols), lambda i: (0, 0, i))
    flip = lambda value: np.ascontiguousarray(value.T)
    input_grad = pl.pallas_call(
        functools.partial(final_kernel, n_axial),
        grid=(steps,),
        in_specs=[
            whole(channels, channels),
            strip,
            whole(2 * KA, LANES), whole(2 * KA, LANES),
            whole(*cos_high.shape), whole(*cos_high.shape),
            whole(n_axial, lines // 2, lanes),
        ],
        out_specs=strip,
        out_shape=jax.ShapeDtypeStruct((channels, rad_rows, ax_cols), BF),
        scratch_shapes=[
            pltpu.VMEM((lines, lines + 2 * KA), BF),
            pltpu.VMEM((2 * KA, ax_cols), BF),
        ],
        compiler_params=params(),
        name="input_gradient",
    )(pointwise_weight, grad_pre, flip(cos_low), flip(sin_low), cos_high, sin_high, gathered)
    return (input_grad, spectral_grad, weight_grad)


def solution(mesh):
    field = P(None, "radial", ("parts", "axial"))
    return jax.shard_map(
        body,
        mesh=mesh,
        in_specs=(field, field, field, P(), P("radial", "axial", None, None)),
        out_specs=(field, P("radial", ("parts", "axial"), None, None), P("parts", None)),
        check_vma=False,
    )
```

```python
import functools
import math

import jax
import jax.numpy as jnp
import numpy as np
from jax import lax
from jax.experimental import pallas as pl
from jax.experimental.pallas import tpu as pltpu
from jax.sharding import PartitionSpec as P

KA = 256
KR = 32
LANES = 128
BF = jnp.bfloat16
F32 = jnp.float32
VMEM_LIMIT = 56 * 1024 * 1024


def axial_factors(n_axial, ax_cols):
    total = n_axial * ax_cols
    own = KA // n_axial
    col = np.arange(2 * KA)
    mode = (col // (2 * own)) * own + col % own
    turn = (col // own) % 2
    points = np.arange(LANES)
    low = (points[:, None] * mode[None, :] % total) * (2.0 * np.pi / total)
    starts = np.arange(total // LANES) * LANES
    high = (starts[:, None] * mode[None, :] % total) * (2.0 * np.pi / total)
    high = high + turn[None, :] * (np.pi / 2)
    as32 = lambda value: value.astype(np.float32)
    return as32(np.cos(low)), as32(np.sin(low)), as32(np.cos(high)), as32(np.sin(high))


def split16(value):
    high = value.astype(BF)
    return high, (value - high.astype(F32)).astype(BF)


def gelu_slope(value):
    return 0.5 * (1.0 + lax.erf(value * (1.0 / math.sqrt(2.0)))) + value * jnp.exp(
        -0.5 * value * value
    ) * (1.0 / math.sqrt(2.0 * math.pi))


def radial_matrices(n_radial, rad_rows, rad, group):
    total = n_radial * rad_rows
    shape = (KR * group, group * rad_rows)
    row = lax.broadcasted_iota(jnp.int32, shape, 0)
    col = lax.broadcasted_iota(jnp.int32, shape, 1)
    q = row // group
    freq = q + jnp.where(q >= KR // 2, total - KR, 0)
    point = rad * rad_rows + col % rad_rows
    phase = (freq * point % total).astype(F32) * (2.0 * math.pi / total)
    same = row % group == col // rad_rows
    return jnp.where(same, jnp.cos(phase), 0.0), jnp.where(same, jnp.sin(phase), 0.0)


def comm_kernel(
    n_axial, n_radial, final_scale,
    w_hbm, x_hbm, s_hbm, c_hbm, cl_ref, sl_ref, ch_ref, sh_ref,
    spec_ref, gath_ref, wg_ref, g_hbm,
    w_vmem, x_vmem, s_vmem, c_vmem, g_vmem, table, px_ref, pg_ref, pair_in, q_buf, chip_in, r_buf, r16, rad_in, dx_all, dx32,
    wl_own, wl_pair, wl_chip, wl_rad, fwd, bwd,
    in_sem, out_sem, s_sem, c_sem, ps, pr, cs, cr, rs, rr, ds_, dr, as_, ar, fs, fr, wps, wpr, wcs, wcr, wrs, wrr,
):
    chips = n_axial // 2
    ax = lax.axis_index("axial")
    rad = lax.axis_index("radial")
    chip = ax // 2
    core = ax % 2
    partner = chip * 2 + 1 - core
    own_k = KA // n_axial
    half = 2 * own_k
    q_own, channels, lanes = spec_ref.shape
    cut = channels // 2
    rad_rows, cols = x_vmem.shape[2:]
    points = n_axial * n_radial * rad_rows * cols
    lines = channels * rad_rows
    group = 8
    rows = group * rad_rows
    parts = (pg_ref, px_ref)

    def remote(src, dst, send, recv, where):
        return pltpu.make_async_remote_copy(
            src_ref=src, dst_ref=dst, send_sem=send, recv_sem=recv,
            device_id=where, device_id_type=pl.DeviceIdType.MESH,
        )

    blocks = cut // group
    loads = []
    for i in range(blocks):
        at = pl.ds(i * group, group)
        loads.append(
            (
                pltpu.make_async_copy(s_hbm.at[:, at], s_vmem.at[:, at], s_sem.at[i]),
                pltpu.make_async_copy(c_hbm.at[:, at], c_vmem.at[:, at], c_sem.at[i]),
            )
        )
        for copy in loads[-1]:
            copy.start()
    local = [
        pltpu.make_async_copy(x_hbm, x_vmem, in_sem.at[0]),
        pltpu.make_async_copy(w_hbm, w_vmem, in_sem.at[1]),
    ]
    for copy in local:
        copy.start()
    peers = [(chip + t) % chips for t in range(chips)]
    rads = [(rad + t) % n_radial for t in range(n_radial)]
    barrier = pltpu.get_barrier_semaphore()
    greet = [{"axial": partner}]
    greet += [{"axial": peers[t] * 2 + core} for t in range(1, chips)]
    greet += [{"radial": rads[t]} for t in range(1, n_radial)]
    for where in greet:
        pl.semaphore_signal(barrier, inc=1, device_id=where, device_id_type=pl.DeviceIdType.MESH)

    pieces = cols // LANES
    for u in range(pieces):
        at = pl.ds(ax * pieces + u, 1)
        table[u * LANES : (u + 1) * LANES, :] = (
            ch_ref[at, :] * cl_ref[...] - sh_ref[at, :] * sl_ref[...]
        ).astype(BF)
    cos_m, sin_m = radial_matrices(n_radial, rad_rows, rad, group)
    both = jnp.concatenate([cos_m, sin_m], axis=1)
    high, low = split16(both)
    fwd[...] = jnp.concatenate([high, high, low], axis=1)
    both = jnp.concatenate([cos_m.T, sin_m.T], axis=1)
    high, low = split16(both)
    bwd[...] = jnp.concatenate([high, low], axis=1)
    waves = table[...]

    def spread(field, out_ref, i):
        block = field[:, i * group : (i + 1) * group].reshape(2 * rows, cols)
        value = jnp.dot(block, waves, preferred_element_type=F32)
        for d in range(n_axial):
            at = slice(d * half, (d + 1) * half)
            out_ref[d, i * rows : (i + 1) * rows, :] = jnp.concatenate(
                [value[:rows, at], value[rows:, at]], axis=1
            ).astype(BF)

    for i in range(blocks):
        for copy in loads[i]:
            copy.wait()
        at = slice(i * group, (i + 1) * group)
        for h in range(2):
            slope = gelu_slope(s_vmem[h, at].astype(F32))
            g_vmem[h, at] = (c_vmem[h, at].astype(F32) * slope).astype(BF)
        spread(g_vmem, pg_ref, i)
    grad_copy = pltpu.make_async_copy(g_vmem, g_hbm, out_sem)
    grad_copy.start()
    pl.semaphore_wait(barrier, len(greet))

    sent = []
    order = list(range(1, chips)) + [0]
    pair = {}
    chip_copies = {}
    for f in range(2):
        if f == 1:
            local[0].wait()
            for i in range(blocks):
                spread(x_vmem, px_ref, i)
        for t in order:
            pair[f, t] = remote(
                parts[f].at[peers[t] * 2 + 1 - core], pair_in.at[f, t], ps.at[f, t], pr.at[f, t],
                {"axial": partner},
            )
            pair[f, t].start()
        for t in order[:-1]:
            pair[f, t].wait_recv()
            q_buf[f, t - 1] = (
                parts[f][peers[t] * 2 + core].astype(F32) + pair_in[f, t].astype(F32)
            ).astype(BF)
            chip_copies[f, t] = remote(
                q_buf.at[f, t - 1], chip_in.at[f, t - 1], cs.at[f, t - 1], cr.at[f, t - 1],
                {"axial": peers[t] * 2 + core},
            )
            chip_copies[f, t].start()
        pair[f, 0].wait_recv()
    sent += list(pair.values()) + list(chip_copies.values())

    def transform(f):
        for t in range(1, chips):
            chip_copies[f, t].wait_recv()
        forward = fwd[...]

        for i in range(cut // group):
            at = pl.ds(i * rows, rows)
            z = parts[f][ax, at, :].astype(F32) + pair_in[f, 0, at, :].astype(F32)
            for t in range(chips - 1):
                z = z + chip_in[f, t, at, :].astype(F32)
            turned = jnp.concatenate(
                [z[:, own_k:half], -z[:, :own_k], z[:, half + own_k :], -z[:, half : half + own_k]],
                axis=1,
            )
            zh, zl = split16(z)
            th, tl = split16(turned)
            stack = jnp.concatenate([zh, th, zl, tl, zh, th], axis=0)
            out = jnp.dot(forward, stack, preferred_element_type=F32)
            r_buf[f, :, i * group : (i + 1) * group, :] = out.reshape(KR, group, lanes)
        copies = []
        for t in range(1, n_radial):
            r16[f, t - 1] = r_buf[f, pl.ds(rads[t] * q_own, q_own)].astype(BF)
            copy = remote(
                r16.at[f, t - 1], rad_in.at[f, t - 1], rs.at[f, t - 1], rr.at[f, t - 1],
                {"radial": rads[t]},
            )
            copy.start()
            copies.append(copy)
        return copies

    def collect(f, q):
        value = r_buf[f, rad * q_own + q]
        for t in range(n_radial - 1):
            value = value + rad_in[f, t, q].astype(F32)
        return jnp.concatenate([value[:, :half], value[:, half:]], axis=0)

    rad_g = transform(0)

    piece = 256
    per = piece // rad_rows
    grads = g_vmem[...].reshape(lines, cols)

    def gram(i, carry):
        block = x_vmem[i // (cut // per), pl.ds(i % (cut // per) * per, per)].reshape(piece, cols)
        full = lax.dot_general(block, grads, (((1,), (1,)), ((), ())), preferred_element_type=F32)
        full = full.reshape(per, rad_rows, lines)
        row = lax.broadcasted_iota(jnp.int32, full.shape, 1)
        col = lax.broadcasted_iota(jnp.int32, full.shape, 2) % rad_rows
        picked = jnp.sum(jnp.where(row == col, full, 0.0), axis=1)
        line = lax.broadcasted_iota(jnp.int32, (lines, channels), 0) // rad_rows
        chan = lax.broadcasted_iota(jnp.int32, (lines, channels), 1)
        chooser = jnp.where(line == chan, 1.0, 0.0).astype(F32)
        wl_own[pl.ds(pl.multiple_of(i * per, per), per), :] = jnp.dot(
            picked, chooser, preferred_element_type=F32, precision=lax.Precision.HIGHEST
        )
        return carry

    lax.fori_loop(0, lines // piece, gram, 0)
    wl_first = remote(wl_own, wl_pair, wps, wpr, {"axial": partner})
    wl_first.start()

    rad_x = transform(1)
    sent += rad_g + rad_x + [wl_first]
    wl_first.wait_recv()
    wl_chip[chip] = wl_own[...] + wl_pair[...]
    wl_copies = []
    for t in range(1, chips):
        copy = remote(
            wl_chip.at[chip], wl_chip.at[chip], wcs.at[t - 1], wcr.at[t - 1],
            {"axial": peers[t] * 2 + core},
        )
        copy.start()
        wl_copies.append(copy)
    sent += wl_copies

    local[1].wait()
    for copy in rad_g:
        copy.wait_recv()

    mode = lax.broadcasted_iota(jnp.int32, (channels, half), 1) % own_k + ax * own_k
    scale = jnp.where(mode == 0, 1.0 / points, 2.0 / points)

    def modes(q, carry):
        g = collect(0, q) * scale
        spec_ref[q, :, half:] = g
        turned = jnp.concatenate([g[:, own_k:], -g[:, :own_k]], axis=1)
        gh, gl = split16(g)
        th, tl = split16(turned)
        side = jnp.concatenate(
            [jnp.concatenate([gh, gl], axis=1), jnp.concatenate([th, tl], axis=1)], axis=0
        )
        out = jnp.dot(
            w_vmem[q].reshape(own_k * channels, 2 * channels), side, preferred_element_type=F32
        )
        lane = lax.broadcasted_iota(jnp.int32, (channels, lanes), 1) % own_k
        total = jnp.zeros((channels, lanes), F32)
        for k in range(own_k):
            total = jnp.where(lane == k, out[k * channels : (k + 1) * channels], total)
        dx = total[:, :half] + total[:, half:]
        dx_all[rad, q] = jnp.concatenate([dx[:cut], dx[cut:]], axis=1).astype(BF)
        return carry

    lax.fori_loop(0, q_own, modes, 0)
    dx_copies = []
    for t in range(1, n_radial):
        copy = remote(dx_all.at[rad], dx_all.at[rad], ds_.at[t - 1], dr.at[t - 1], {"radial": rads[t]})
        copy.start()
        dx_copies.append(copy)
    sent += dx_copies

    for copy in wl_copies:
        copy.wait_recv()
    total = wl_chip[0]
    for t in range(1, chips):
        total = total + wl_chip[t]
    wl_rad[rad] = total
    wl_rad_copies = []
    for t in range(1, n_radial):
        copy = remote(
            wl_rad.at[rad], wl_rad.at[rad], wrs.at[t - 1], wrr.at[t - 1], {"radial": rads[t]}
        )
        copy.start()
        wl_rad_copies.append(copy)
    sent += wl_rad_copies

    for copy in dx_copies:
        copy.wait_recv()
    for t in range(n_radial):
        dx32[t * q_own : (t + 1) * q_own] = dx_all[t].astype(F32)
    backward = bwd[...]
    for i in range(cut // group):
        d = dx32[:, i * group : (i + 1) * group, :].reshape(KR * group, lanes)
        turned = jnp.concatenate(
            [-d[:, own_k:half], d[:, :own_k], -d[:, half + own_k :], d[:, half : half + own_k]], axis=1
        )
        d16 = d.astype(BF)
        t16 = turned.astype(BF)
        stack = jnp.concatenate([d16, t16, d16, t16], axis=0)
        gath_ref[ax, i * rows : (i + 1) * rows, :] = jnp.dot(
            backward, stack, preferred_element_type=F32
        ).astype(BF)
    gather = []
    for t in range(1, chips):
        copy = remote(
            gath_ref.at[ax], gath_ref.at[ax], as_.at[t - 1], ar.at[t - 1], {"axial": peers[t] * 2 + core}
        )
        copy.start()
        gather.append(copy)
    passed = [remote(gath_ref.at[ax], gath_ref.at[ax], fs.at[0], fr.at[0], {"axial": partner})]
    passed[0].start()

    for copy in rad_x:
        copy.wait_recv()

    def keep(q, carry):
        spec_ref[q, :, :half] = collect(1, q)
        return carry

    lax.fori_loop(0, q_own, keep, 0)
    for t in range(1, chips):
        gather[t - 1].wait_recv()
        slot = ((chip - t + chips) % chips) * 2 + core
        copy = remote(gath_ref.at[slot], gath_ref.at[slot], fs.at[t], fr.at[t], {"axial": partner})
        copy.start()
        passed.append(copy)

    for copy in wl_rad_copies:
        copy.wait_recv()
    total = wl_rad[0]
    for t in range(1, n_radial):
        total = total + wl_rad[t]
    wg_ref[...] = total * final_scale

    for copy in passed:
        copy.wait_recv()
    for copy in sent + gather + passed:
        copy.wait_send()
    grad_copy.wait()


def mode_products(own_k, value, out_ref):
    half = 2 * own_k
    channels = value.shape[0]
    xh, xl = split16(value[:, :half])
    left = jnp.concatenate([xh, xl, xh], axis=1).reshape(channels // 16, 16, 3 * half)
    turned = jnp.transpose(value[:, half:])
    real, imag = turned[:own_k], turned[own_k:]
    sides = jnp.concatenate(
        [jnp.concatenate([real, imag], axis=1), jnp.concatenate([imag, -real], axis=1)], axis=0
    )
    sh, sl = split16(sides)
    right = jnp.concatenate([sh, sh, sl], axis=0)
    lane = lax.broadcasted_iota(jnp.int32, (16, 3 * half), 1) % own_k
    together = 8
    for first in range(0, own_k, together):
        rows = []
        for k in range(first, first + together):
            mask = jnp.where(lane == k, 1.0, 0.0).astype(BF)
            rows.append((left * mask[None]).reshape(channels, 3 * half))
        out = jnp.dot(jnp.concatenate(rows, axis=0), right, preferred_element_type=F32)
        out_ref[first : first + together] = out.reshape(together, channels, 2 * channels)


def final_kernel(
    n_axial, pw_ref, grad_ref, cl_ref, sl_ref, ch_ref, sh_ref, gath_ref, spec_ref, wg_ref,
    out_ref, modes_hbm, wg_out, left, table, modes_vmem, mode_sem,
):
    channels, rad_rows, cols = grad_ref.shape
    lines = channels * rad_rows
    half = 2 * KA // n_axial
    pieces = table.shape[1] // LANES
    step = pl.program_id(0)
    q_own = spec_ref.shape[0]

    def store(q):
        return pltpu.make_async_copy(modes_vmem.at[q], modes_hbm.at[q], mode_sem.at[q])

    @pl.when(step == 0)
    def _():
        def products(q, carry):
            mode_products(KA // n_axial, spec_ref[q], modes_vmem.at[q])
            store(q).start()
            return carry

        lax.fori_loop(0, q_own, products, 0)
        wg_out[...] = wg_ref[...]
        line = lax.broadcasted_iota(jnp.int32, (lines, channels), 0) // rad_rows
        chan = lax.broadcasted_iota(jnp.int32, (lines, channels), 1)
        chooser = jnp.where(line == chan, 1.0, 0.0).astype(BF)
        rows = jnp.dot(chooser, pw_ref[...], preferred_element_type=F32).astype(BF)
        dims = (((1,), (1,)), ((), ()))
        wide = lax.dot_general(rows, chooser, dims, preferred_element_type=F32)
        row = lax.broadcasted_iota(jnp.int32, wide.shape, 0) % rad_rows
        col = lax.broadcasted_iota(jnp.int32, wide.shape, 1) % rad_rows
        left[:, :lines] = jnp.where(row == col, wide, 0.0).astype(BF)
        cut = lines // 2
        for d in range(n_axial):
            lanes = slice(lines + d * half, lines + (d + 1) * half)
            left[:cut, lanes] = gath_ref[d, :, :half]
            left[cut:, lanes] = gath_ref[d, :, half:]
        first = pl.multiple_of(lax.axis_index("axial") * pieces, pieces)
        cos_high = jnp.transpose(ch_ref[pl.ds(first, pieces), :])
        sin_high = jnp.transpose(sh_ref[pl.ds(first, pieces), :])
        for u in range(pieces):
            table[:, u * LANES : (u + 1) * LANES] = (
                cos_high[:, u : u + 1] * cl_ref[...] - sin_high[:, u : u + 1] * sl_ref[...]
            ).astype(BF)

    waves = table[:, pl.ds(pl.multiple_of(step * cols, cols), cols)]
    right = jnp.concatenate([grad_ref[...].reshape(lines, cols), waves], axis=0)
    value = jnp.dot(left[...], right, preferred_element_type=F32)
    out_ref[...] = value.astype(BF).reshape(channels, rad_rows, cols)

    @pl.when(step == pl.num_programs(0) - 1)
    def _():
        for q in range(q_own):
            store(q).wait()


def params(**more):
    return pltpu.CompilerParams(vmem_limit_bytes=VMEM_LIMIT, **more)


def body(inputs, saved_pre, cotangent, pointwise_weight, spectral_weight):
    channels, rad_rows, ax_cols = inputs.shape
    n_axial = lax.axis_size("axial")
    n_radial = lax.axis_size("radial")
    points = ax_cols * n_axial * rad_rows * n_radial
    own_k = KA // n_axial
    q_own = KR // n_radial
    lines = channels * rad_rows
    lanes = 4 * own_k
    chips = n_axial // 2
    cut = channels // 2

    cos_low, sin_low, cos_high, sin_high = axial_factors(n_axial, ax_cols)
    whole = lambda *shape: pl.BlockSpec(shape, lambda i: (0,) * len(shape))
    group = 8
    halves = lambda value: value.reshape(2, cut, rad_rows, ax_cols)
    split = (2, cut, rad_rows, ax_cols)
    vmem = pl.BlockSpec(memory_space=pltpu.VMEM)
    hbm = pl.BlockSpec(memory_space=pl.ANY)
    dma = lambda *count: pltpu.SemaphoreType.DMA(count)
    one = pltpu.SemaphoreType.DMA
    spec, gathered, weight_grad, grad_pre = pl.pallas_call(
        functools.partial(comm_kernel, n_axial, n_radial, 1.0 / math.sqrt(points)),
        in_specs=[hbm, hbm, hbm, hbm, vmem, vmem, vmem, vmem],
        out_specs=[vmem, vmem, vmem, hbm],
        out_shape=[
            jax.ShapeDtypeStruct((q_own, channels, lanes), F32),
            jax.ShapeDtypeStruct((n_axial, lines // 2, lanes), BF),
            jax.ShapeDtypeStruct((channels, channels), F32),
            jax.ShapeDtypeStruct(split, BF),
        ],
        scratch_shapes=[
            pltpu.VMEM(spectral_weight.shape, BF),
            pltpu.VMEM(split, BF),
            pltpu.VMEM(split, BF),
            pltpu.VMEM(split, BF),
            pltpu.VMEM(split, BF),
            pltpu.VMEM((ax_cols, 2 * KA), BF),
            pltpu.VMEM((n_axial, lines // 2, lanes), BF),
            pltpu.VMEM((n_axial, lines // 2, lanes), BF),
            pltpu.VMEM((2, chips, lines // 2, lanes), BF),
            pltpu.VMEM((2, chips - 1, lines // 2, lanes), BF),
            pltpu.VMEM((2, chips - 1, lines // 2, lanes), BF),
            pltpu.VMEM((2, KR, cut, lanes), F32),
            pltpu.VMEM((2, n_radial - 1, q_own, cut, lanes), BF),
            pltpu.VMEM((2, n_radial - 1, q_own, cut, lanes), BF),
            pltpu.VMEM((n_radial, q_own, cut, lanes), BF),
            pltpu.VMEM((KR, cut, lanes), F32),
            pltpu.VMEM((channels, channels), F32),
            pltpu.VMEM((channels, channels), F32),
            pltpu.VMEM((chips, channels, channels), F32),
            pltpu.VMEM((n_radial, channels, channels), F32),
            pltpu.VMEM((KR * group, 6 * group * rad_rows), BF),
            pltpu.VMEM((group * rad_rows, 4 * KR * group), BF),
            dma(2), one, dma(cut // group), dma(cut // group),
            dma(2, chips), dma(2, chips),
            dma(2, chips - 1), dma(2, chips - 1),
            dma(2, n_radial - 1), dma(2, n_radial - 1),
            dma(n_radial - 1), dma(n_radial - 1),
            dma(chips - 1), dma(chips - 1),
            dma(chips), dma(chips),
            one, one,
            dma(chips - 1), dma(chips - 1),
            dma(n_radial - 1), dma(n_radial - 1),
        ],
        compiler_params=params(collective_id=0, has_side_effects=True),
        name="exchange",
    )(
        spectral_weight, halves(inputs), halves(saved_pre), halves(cotangent),
        cos_low, sin_low, cos_high, sin_high,
    )
    grad_pre = grad_pre.reshape(channels, rad_rows, ax_cols)

    steps = 4
    cols = ax_cols // steps
    strip = pl.BlockSpec((channels, rad_rows, cols), lambda i: (0, 0, i))
    flip = lambda value: np.ascontiguousarray(value.T)
    input_grad, spectral_grad, weight_grad = pl.pallas_call(
        functools.partial(final_kernel, n_axial),
        grid=(steps,),
        in_specs=[
            whole(channels, channels),
            strip,
            whole(2 * KA, LANES), whole(2 * KA, LANES),
            whole(*cos_high.shape), whole(*cos_high.shape),
            whole(n_axial, lines // 2, lanes),
            whole(q_own, channels, lanes),
            whole(channels, channels),
        ],
        out_specs=[strip, hbm, whole(channels, channels)],
        out_shape=[
            jax.ShapeDtypeStruct((channels, rad_rows, ax_cols), BF),
            jax.ShapeDtypeStruct((q_own, own_k, channels, 2 * channels), F32),
            jax.ShapeDtypeStruct((channels, channels), F32),
        ],
        scratch_shapes=[
            pltpu.VMEM((lines, lines + 2 * KA), BF),
            pltpu.VMEM((2 * KA, ax_cols), BF),
            pltpu.VMEM((q_own, own_k, channels, 2 * channels), F32),
            dma(q_own),
        ],
        compiler_params=params(),
        name="input_gradient",
    )(pointwise_weight, grad_pre, flip(cos_low), flip(sin_low), cos_high, sin_high, gathered, spec, weight_grad)
    return (input_grad, spectral_grad, weight_grad)


def solution(mesh):
    field = P(None, "radial", ("parts", "axial"))
    return jax.shard_map(
        body,
        mesh=mesh,
        in_specs=(field, field, field, P(), P("radial", "axial", None, None)),
        out_specs=(field, P("radial", ("parts", "axial"), None, None), P("parts", None)),
        check_vma=False,
    )
```

```python
import functools
import math

import jax
import jax.numpy as jnp
import numpy as np
from jax import lax
from jax.experimental import pallas as pl
from jax.experimental.pallas import tpu as pltpu
from jax.sharding import PartitionSpec as P

KA = 256
KR = 32
LANES = 128
BF = jnp.bfloat16
F32 = jnp.float32
VMEM_LIMIT = 56 * 1024 * 1024


def axial_factors(n_axial, ax_cols):
    total = n_axial * ax_cols
    own = KA // n_axial
    col = np.arange(2 * KA)
    mode = (col // (2 * own)) * own + col % own
    turn = (col // own) % 2
    points = np.arange(LANES)
    low = (points[:, None] * mode[None, :] % total) * (2.0 * np.pi / total)
    starts = np.arange(total // LANES) * LANES
    high = (starts[:, None] * mode[None, :] % total) * (2.0 * np.pi / total)
    high = high + turn[None, :] * (np.pi / 2)
    as32 = lambda value: value.astype(np.float32)
    return as32(np.cos(low)), as32(np.sin(low)), as32(np.cos(high)), as32(np.sin(high))


def rest_of(value, size):
    return value & (size - 1) if size & (size - 1) == 0 else value % size


def part_of(value, size):
    return value >> (size.bit_length() - 1) if size & (size - 1) == 0 else value // size


def same_row(rad_rows, lines):
    row = lax.broadcasted_iota(jnp.int32, (rad_rows, lines), 0)
    return row == rest_of(lax.broadcasted_iota(jnp.int32, (rad_rows, lines), 1), rad_rows)


def chooser_of(lines, channels, rad_rows, kind):
    line = part_of(lax.broadcasted_iota(jnp.int32, (lines, channels), 0), rad_rows)
    chan = lax.broadcasted_iota(jnp.int32, (lines, channels), 1)
    return jnp.where(line == chan, 1.0, 0.0).astype(kind)


def split16(value):
    high = value.astype(BF)
    return high, (value - high.astype(F32)).astype(BF)


def gelu_slope(value):
    return 0.5 * (1.0 + lax.erf(value * (1.0 / math.sqrt(2.0)))) + value * jnp.exp(
        -0.5 * value * value
    ) * (1.0 / math.sqrt(2.0 * math.pi))


def radial_matrices(n_radial, rad_rows, rad, group):
    total = n_radial * rad_rows
    shape = (KR * group, group * rad_rows)
    row = lax.broadcasted_iota(jnp.int32, shape, 0)
    col = lax.broadcasted_iota(jnp.int32, shape, 1)
    q = part_of(row, group)
    freq = q + jnp.where(q >= KR // 2, total - KR, 0)
    point = rad * rad_rows + rest_of(col, rad_rows)
    phase = rest_of(freq * point, total).astype(F32) * (2.0 * math.pi / total)
    same = rest_of(row, group) == part_of(col, rad_rows)
    return jnp.where(same, jnp.cos(phase), 0.0), jnp.where(same, jnp.sin(phase), 0.0)


def comm_kernel(
    n_axial, n_radial, final_scale,
    w_hbm, x_hbm, s_hbm, c_hbm, cl_ref, sl_ref, ch_ref, sh_ref,
    spec_ref, gath_ref, wg_ref, g_hbm,
    w_vmem, x_vmem, s_vmem, c_vmem, g_vmem, table, px_ref, pg_ref, pair_in, q_buf, chip_in, r_buf, r16, rad_in, dx_all, dx32,
    wl_own, wl_pair, wl_chip, wl_rad, fwd, bwd,
    in_sem, out_sem, s_sem, c_sem, ps, pr, cs, cr, rs, rr, ds_, dr, as_, ar, fs, fr, wps, wpr, wcs, wcr, wrs, wrr,
):
    chips = n_axial // 2
    ax = lax.axis_index("axial")
    rad = lax.axis_index("radial")
    chip = ax // 2
    core = ax % 2
    partner = chip * 2 + 1 - core
    own_k = KA // n_axial
    half = 2 * own_k
    q_own, channels, lanes = spec_ref.shape
    cut = channels // 2
    rad_rows, cols = x_vmem.shape[2:]
    points = n_axial * n_radial * rad_rows * cols
    lines = channels * rad_rows
    group = 8
    rows = group * rad_rows
    parts = (pg_ref, px_ref)

    def remote(src, dst, send, recv, where):
        return pltpu.make_async_remote_copy(
            src_ref=src, dst_ref=dst, send_sem=send, recv_sem=recv,
            device_id=where, device_id_type=pl.DeviceIdType.MESH,
        )

    blocks = cut // group
    loads = []
    for i in range(blocks):
        at = pl.ds(i * group, group)
        loads.append(
            (
                pltpu.make_async_copy(s_hbm.at[:, at], s_vmem.at[:, at], s_sem.at[i]),
                pltpu.make_async_copy(c_hbm.at[:, at], c_vmem.at[:, at], c_sem.at[i]),
            )
        )
        for copy in loads[-1]:
            copy.start()
    local = [
        pltpu.make_async_copy(x_hbm, x_vmem, in_sem.at[0]),
        pltpu.make_async_copy(w_hbm, w_vmem, in_sem.at[1]),
    ]
    for copy in local:
        copy.start()
    peers = [(chip + t) % chips for t in range(chips)]
    rads = [(rad + t) % n_radial for t in range(n_radial)]
    barrier = pltpu.get_barrier_semaphore()
    greet = [{"axial": partner}]
    greet += [{"axial": peers[t] * 2 + core} for t in range(1, chips)]
    greet += [{"radial": rads[t]} for t in range(1, n_radial)]
    for where in greet:
        pl.semaphore_signal(barrier, inc=1, device_id=where, device_id_type=pl.DeviceIdType.MESH)

    pieces = cols // LANES
    for u in range(pieces):
        at = pl.ds(ax * pieces + u, 1)
        table[u * LANES : (u + 1) * LANES, :] = (
            ch_ref[at, :] * cl_ref[...] - sh_ref[at, :] * sl_ref[...]
        ).astype(BF)
    cos_m, sin_m = radial_matrices(n_radial, rad_rows, rad, group)
    both = jnp.concatenate([cos_m, sin_m], axis=1)
    high, low = split16(both)
    fwd[...] = jnp.concatenate([high, high, low], axis=1)
    both = jnp.concatenate([cos_m.T, sin_m.T], axis=1)
    high, low = split16(both)
    bwd[...] = jnp.concatenate([high, low], axis=1)
    waves = table[...]

    def spread(field, out_ref, i):
        block = field[:, i * group : (i + 1) * group].reshape(2 * rows, cols)
        value = jnp.dot(block, waves, preferred_element_type=F32)
        for d in range(n_axial):
            at = slice(d * half, (d + 1) * half)
            out_ref[d, i * rows : (i + 1) * rows, :] = jnp.concatenate(
                [value[:rows, at], value[rows:, at]], axis=1
            ).astype(BF)

    for i in range(blocks):
        for copy in loads[i]:
            copy.wait()
        at = slice(i * group, (i + 1) * group)
        for h in range(2):
            slope = gelu_slope(s_vmem[h, at].astype(F32))
            g_vmem[h, at] = (c_vmem[h, at].astype(F32) * slope).astype(BF)
        spread(g_vmem, pg_ref, i)
    grad_copy = pltpu.make_async_copy(g_vmem, g_hbm, out_sem)
    grad_copy.start()
    pl.semaphore_wait(barrier, len(greet))

    sent = []
    order = list(range(1, chips)) + [0]
    pair = {}
    chip_copies = {}
    for f in range(2):
        if f == 1:
            local[0].wait()
            for i in range(blocks):
                spread(x_vmem, px_ref, i)
        for t in order:
            pair[f, t] = remote(
                parts[f].at[peers[t] * 2 + 1 - core], pair_in.at[f, t], ps.at[f, t], pr.at[f, t],
                {"axial": partner},
            )
            pair[f, t].start()
        for t in order[:-1]:
            pair[f, t].wait_recv()
            q_buf[f, t - 1] = (
                parts[f][peers[t] * 2 + core].astype(F32) + pair_in[f, t].astype(F32)
            ).astype(BF)
            chip_copies[f, t] = remote(
                q_buf.at[f, t - 1], chip_in.at[f, t - 1], cs.at[f, t - 1], cr.at[f, t - 1],
                {"axial": peers[t] * 2 + core},
            )
            chip_copies[f, t].start()
        pair[f, 0].wait_recv()
    sent += list(pair.values()) + list(chip_copies.values())

    def transform(f):
        for t in range(1, chips):
            chip_copies[f, t].wait_recv()
        forward = fwd[...]

        for i in range(cut // group):
            at = pl.ds(i * rows, rows)
            z = parts[f][ax, at, :].astype(F32) + pair_in[f, 0, at, :].astype(F32)
            for t in range(chips - 1):
                z = z + chip_in[f, t, at, :].astype(F32)
            turned = jnp.concatenate(
                [z[:, own_k:half], -z[:, :own_k], z[:, half + own_k :], -z[:, half : half + own_k]],
                axis=1,
            )
            zh, zl = split16(z)
            th, tl = split16(turned)
            stack = jnp.concatenate([zh, th, zl, tl, zh, th], axis=0)
            out = jnp.dot(forward, stack, preferred_element_type=F32)
            r_buf[f, :, i * group : (i + 1) * group, :] = out.reshape(KR, group, lanes)
        copies = []
        for t in range(1, n_radial):
            r16[f, t - 1] = r_buf[f, pl.ds(rads[t] * q_own, q_own)].astype(BF)
            copy = remote(
                r16.at[f, t - 1], rad_in.at[f, t - 1], rs.at[f, t - 1], rr.at[f, t - 1],
                {"radial": rads[t]},
            )
            copies.append(copy)
        return copies

    def collect(f, q):
        value = r_buf[f, rad * q_own + q]
        for t in range(n_radial - 1):
            value = value + rad_in[f, t, q].astype(F32)
        return jnp.concatenate([value[:, :half], value[:, half:]], axis=0)

    rad_g = transform(0)
    for copy in rad_g:
        copy.start()

    piece = 256
    per = piece // rad_rows
    grads = g_vmem[...].reshape(lines, cols)
    chooser = chooser_of(lines, channels, rad_rows, F32)
    match = same_row(rad_rows, lines)

    def gram(i, carry):
        block = x_vmem[i // (cut // per), pl.ds(i % (cut // per) * per, per)].reshape(piece, cols)
        full = lax.dot_general(block, grads, (((1,), (1,)), ((), ())), preferred_element_type=F32)
        full = full.reshape(per, rad_rows, lines)
        picked = jnp.sum(jnp.where(match[None], full, 0.0), axis=1)
        wl_own[pl.ds(pl.multiple_of(i * per, per), per), :] = jnp.dot(
            picked, chooser, preferred_element_type=F32, precision=lax.Precision.HIGHEST
        )
        return carry

    lax.fori_loop(0, lines // piece, gram, 0)
    wl_first = remote(wl_own, wl_pair, wps, wpr, {"axial": partner})
    wl_first.start()

    rad_x = transform(1)
    sent += rad_g + rad_x + [wl_first]
    wl_first.wait_recv()
    wl_chip[chip] = wl_own[...] + wl_pair[...]
    wl_copies = []
    for t in range(1, chips):
        copy = remote(
            wl_chip.at[chip], wl_chip.at[chip], wcs.at[t - 1], wcr.at[t - 1],
            {"axial": peers[t] * 2 + core},
        )
        copy.start()
        wl_copies.append(copy)
    sent += wl_copies

    local[1].wait()
    for copy in rad_g:
        copy.wait_recv()

    mode = rest_of(lax.broadcasted_iota(jnp.int32, (channels, half), 1), own_k) + ax * own_k
    scale = jnp.where(mode == 0, 1.0 / points, 2.0 / points)

    lane = rest_of(lax.broadcasted_iota(jnp.int32, (channels, lanes), 1), own_k)
    pairs = 2 if q_own % 2 == 0 else 1

    def modes(step, carry):
        sides = [dy_side(step * pairs + j) for j in range(pairs)]
        for j in range(pairs):
            mode_back(step * pairs + j, sides[j])
        return carry

    def dy_side(q):
        g = collect(0, q) * scale
        spec_ref[q, :, half:] = g
        turned = jnp.concatenate([g[:, own_k:], -g[:, :own_k]], axis=1)
        gh, gl = split16(g)
        th, tl = split16(turned)
        return jnp.concatenate(
            [jnp.concatenate([gh, gl], axis=1), jnp.concatenate([th, tl], axis=1)], axis=0
        )

    def mode_back(q, side):
        out = jnp.dot(
            w_vmem[q].reshape(own_k * channels, 2 * channels), side, preferred_element_type=F32
        )
        total = jnp.zeros((channels, lanes), F32)
        for k in range(own_k):
            total = jnp.where(lane == k, out[k * channels : (k + 1) * channels], total)
        dx = total[:, :half] + total[:, half:]
        dx_all[rad, q] = jnp.concatenate([dx[:cut], dx[cut:]], axis=1).astype(BF)

    lax.fori_loop(0, q_own // pairs, modes, 0)
    dx_copies = []
    for t in range(1, n_radial):
        copy = remote(dx_all.at[rad], dx_all.at[rad], ds_.at[t - 1], dr.at[t - 1], {"radial": rads[t]})
        copy.start()
        dx_copies.append(copy)
    sent += dx_copies
    for copy in rad_x:
        copy.start()

    for copy in wl_copies:
        copy.wait_recv()
    total = wl_chip[0]
    for t in range(1, chips):
        total = total + wl_chip[t]
    wl_rad[rad] = total
    wl_rad_copies = []
    for t in range(1, n_radial):
        copy = remote(
            wl_rad.at[rad], wl_rad.at[rad], wrs.at[t - 1], wrr.at[t - 1], {"radial": rads[t]}
        )
        copy.start()
        wl_rad_copies.append(copy)
    sent += wl_rad_copies

    for copy in dx_copies:
        copy.wait_recv()
    for t in range(n_radial):
        dx32[t * q_own : (t + 1) * q_own] = dx_all[t].astype(F32)
    backward = bwd[...]
    for i in range(cut // group):
        d = dx32[:, i * group : (i + 1) * group, :].reshape(KR * group, lanes)
        turned = jnp.concatenate(
            [-d[:, own_k:half], d[:, :own_k], -d[:, half + own_k :], d[:, half : half + own_k]], axis=1
        )
        d16 = d.astype(BF)
        t16 = turned.astype(BF)
        stack = jnp.concatenate([d16, t16, d16, t16], axis=0)
        gath_ref[ax, i * rows : (i + 1) * rows, :] = jnp.dot(
            backward, stack, preferred_element_type=F32
        ).astype(BF)
    gather = []
    for t in range(1, chips):
        copy = remote(
            gath_ref.at[ax], gath_ref.at[ax], as_.at[t - 1], ar.at[t - 1], {"axial": peers[t] * 2 + core}
        )
        copy.start()
        gather.append(copy)
    passed = [remote(gath_ref.at[ax], gath_ref.at[ax], fs.at[0], fr.at[0], {"axial": partner})]
    passed[0].start()

    for copy in rad_x:
        copy.wait_recv()

    def keep(q, carry):
        spec_ref[q, :, :half] = collect(1, q)
        return carry

    lax.fori_loop(0, q_own, keep, 0)
    for t in range(1, chips):
        gather[t - 1].wait_recv()
        slot = ((chip - t + chips) % chips) * 2 + core
        copy = remote(gath_ref.at[slot], gath_ref.at[slot], fs.at[t], fr.at[t], {"axial": partner})
        copy.start()
        passed.append(copy)

    for copy in wl_rad_copies:
        copy.wait_recv()
    total = wl_rad[0]
    for t in range(1, n_radial):
        total = total + wl_rad[t]
    wg_ref[...] = total * final_scale

    for copy in passed:
        copy.wait_recv()
    for copy in sent + gather + passed:
        copy.wait_send()
    grad_copy.wait()


def mode_products(own_k, value, out_ref):
    half = 2 * own_k
    channels = value.shape[0]
    xh, xl = split16(value[:, :half])
    left = jnp.concatenate([xh, xl, xh], axis=1).reshape(channels // 16, 16, 3 * half)
    turned = jnp.transpose(value[:, half:])
    real, imag = turned[:own_k], turned[own_k:]
    sides = jnp.concatenate(
        [jnp.concatenate([real, imag], axis=1), jnp.concatenate([imag, -real], axis=1)], axis=0
    )
    sh, sl = split16(sides)
    right = jnp.concatenate([sh, sh, sl], axis=0)
    lane = rest_of(lax.broadcasted_iota(jnp.int32, (16, 3 * half), 1), own_k)
    together = 8
    for first in range(0, own_k, together):
        rows = []
        for k in range(first, first + together):
            mask = jnp.where(lane == k, 1.0, 0.0).astype(BF)
            rows.append((left * mask[None]).reshape(channels, 3 * half))
        out = jnp.dot(jnp.concatenate(rows, axis=0), right, preferred_element_type=F32)
        out_ref[first : first + together] = out.reshape(together, channels, 2 * channels)


def final_kernel(
    n_axial, pw_ref, grad_ref, cl_ref, sl_ref, ch_ref, sh_ref, gath_ref, spec_ref, wg_ref,
    out_ref, modes_hbm, wg_out, left, table, modes_vmem, mode_sem,
):
    channels, rad_rows, cols = grad_ref.shape
    lines = channels * rad_rows
    half = 2 * KA // n_axial
    pieces = table.shape[1] // LANES
    step = pl.program_id(0)
    q_own = spec_ref.shape[0]

    def store(q):
        return pltpu.make_async_copy(modes_vmem.at[q], modes_hbm.at[q], mode_sem.at[q])

    @pl.when(step == 0)
    def _():
        pairs = 2 if q_own % 2 == 0 else 1

        def products(i, carry):
            for j in range(pairs):
                mode_products(KA // n_axial, spec_ref[i * pairs + j], modes_vmem.at[i * pairs + j])
            for j in range(pairs):
                store(i * pairs + j).start()
            return carry

        lax.fori_loop(0, q_own // pairs, products, 0)
        wg_out[...] = wg_ref[...]
        chooser = chooser_of(lines, channels, rad_rows, BF)
        rows = jnp.dot(chooser, pw_ref[...], preferred_element_type=F32).astype(BF)
        dims = (((1,), (1,)), ((), ()))
        wide = lax.dot_general(rows, chooser, dims, preferred_element_type=F32)
        match = same_row(rad_rows, lines)
        wide = jnp.where(match[None], wide.reshape(channels, rad_rows, lines), 0.0)
        left[:, :lines] = wide.reshape(lines, lines).astype(BF)
        cut = lines // 2
        for d in range(n_axial):
            lanes = slice(lines + d * half, lines + (d + 1) * half)
            left[:cut, lanes] = gath_ref[d, :, :half]
            left[cut:, lanes] = gath_ref[d, :, half:]
        first = pl.multiple_of(lax.axis_index("axial") * pieces, pieces)
        cos_high = jnp.transpose(ch_ref[pl.ds(first, pieces), :])
        sin_high = jnp.transpose(sh_ref[pl.ds(first, pieces), :])
        for u in range(pieces):
            table[:, u * LANES : (u + 1) * LANES] = (
                cos_high[:, u : u + 1] * cl_ref[...] - sin_high[:, u : u + 1] * sl_ref[...]
            ).astype(BF)

    waves = table[:, pl.ds(pl.multiple_of(step * cols, cols), cols)]
    right = jnp.concatenate([grad_ref[...].reshape(lines, cols), waves], axis=0)
    value = jnp.dot(left[...], right, preferred_element_type=F32)
    out_ref[...] = value.astype(BF).reshape(channels, rad_rows, cols)

    @pl.when(step == pl.num_programs(0) - 1)
    def _():
        for q in range(q_own):
            store(q).wait()


def params(**more):
    return pltpu.CompilerParams(vmem_limit_bytes=VMEM_LIMIT, **more)


def body(inputs, saved_pre, cotangent, pointwise_weight, spectral_weight):
    channels, rad_rows, ax_cols = inputs.shape
    n_axial = lax.axis_size("axial")
    n_radial = lax.axis_size("radial")
    points = ax_cols * n_axial * rad_rows * n_radial
    own_k = KA // n_axial
    q_own = KR // n_radial
    lines = channels * rad_rows
    lanes = 4 * own_k
    chips = n_axial // 2
    cut = channels // 2

    cos_low, sin_low, cos_high, sin_high = axial_factors(n_axial, ax_cols)
    whole = lambda *shape: pl.BlockSpec(shape, lambda i: (0,) * len(shape))
    group = 8
    halves = lambda value: value.reshape(2, cut, rad_rows, ax_cols)
    split = (2, cut, rad_rows, ax_cols)
    vmem = pl.BlockSpec(memory_space=pltpu.VMEM)
    hbm = pl.BlockSpec(memory_space=pl.ANY)
    dma = lambda *count: pltpu.SemaphoreType.DMA(count)
    one = pltpu.SemaphoreType.DMA
    spec, gathered, weight_grad, grad_pre = pl.pallas_call(
        functools.partial(comm_kernel, n_axial, n_radial, 1.0 / math.sqrt(points)),
        in_specs=[hbm, hbm, hbm, hbm, vmem, vmem, vmem, vmem],
        out_specs=[vmem, vmem, vmem, hbm],
        out_shape=[
            jax.ShapeDtypeStruct((q_own, channels, lanes), F32),
            jax.ShapeDtypeStruct((n_axial, lines // 2, lanes), BF),
            jax.ShapeDtypeStruct((channels, channels), F32),
            jax.ShapeDtypeStruct(split, BF),
        ],
        scratch_shapes=[
            pltpu.VMEM(spectral_weight.shape, BF),
            pltpu.VMEM(split, BF),
            pltpu.VMEM(split, BF),
            pltpu.VMEM(split, BF),
            pltpu.VMEM(split, BF),
            pltpu.VMEM((ax_cols, 2 * KA), BF),
            pltpu.VMEM((n_axial, lines // 2, lanes), BF),
            pltpu.VMEM((n_axial, lines // 2, lanes), BF),
            pltpu.VMEM((2, chips, lines // 2, lanes), BF),
            pltpu.VMEM((2, chips - 1, lines // 2, lanes), BF),
            pltpu.VMEM((2, chips - 1, lines // 2, lanes), BF),
            pltpu.VMEM((2, KR, cut, lanes), F32),
            pltpu.VMEM((2, n_radial - 1, q_own, cut, lanes), BF),
            pltpu.VMEM((2, n_radial - 1, q_own, cut, lanes), BF),
            pltpu.VMEM((n_radial, q_own, cut, lanes), BF),
            pltpu.VMEM((KR, cut, lanes), F32),
            pltpu.VMEM((channels, channels), F32),
            pltpu.VMEM((channels, channels), F32),
            pltpu.VMEM((chips, channels, channels), F32),
            pltpu.VMEM((n_radial, channels, channels), F32),
            pltpu.VMEM((KR * group, 6 * group * rad_rows), BF),
            pltpu.VMEM((group * rad_rows, 4 * KR * group), BF),
            dma(2), one, dma(cut // group), dma(cut // group),
            dma(2, chips), dma(2, chips),
            dma(2, chips - 1), dma(2, chips - 1),
            dma(2, n_radial - 1), dma(2, n_radial - 1),
            dma(n_radial - 1), dma(n_radial - 1),
            dma(chips - 1), dma(chips - 1),
            dma(chips), dma(chips),
            one, one,
            dma(chips - 1), dma(chips - 1),
            dma(n_radial - 1), dma(n_radial - 1),
        ],
        compiler_params=params(collective_id=0, has_side_effects=True),
        name="exchange",
    )(
        spectral_weight, halves(inputs), halves(saved_pre), halves(cotangent),
        cos_low, sin_low, cos_high, sin_high,
    )
    grad_pre = grad_pre.reshape(channels, rad_rows, ax_cols)

    steps = 4
    cols = ax_cols // steps
    strip = pl.BlockSpec((channels, rad_rows, cols), lambda i: (0, 0, i))
    flip = lambda value: np.ascontiguousarray(value.T)
    input_grad, spectral_grad, weight_grad = pl.pallas_call(
        functools.partial(final_kernel, n_axial),
        grid=(steps,),
        in_specs=[
            whole(channels, channels),
            strip,
            whole(2 * KA, LANES), whole(2 * KA, LANES),
            whole(*cos_high.shape), whole(*cos_high.shape),
            whole(n_axial, lines // 2, lanes),
            whole(q_own, channels, lanes),
            whole(channels, channels),
        ],
        out_specs=[strip, hbm, whole(channels, channels)],
        out_shape=[
            jax.ShapeDtypeStruct((channels, rad_rows, ax_cols), BF),
            jax.ShapeDtypeStruct((q_own, own_k, channels, 2 * channels), F32),
            jax.ShapeDtypeStruct((channels, channels), F32),
        ],
        scratch_shapes=[
            pltpu.VMEM((lines, lines + 2 * KA), BF),
            pltpu.VMEM((2 * KA, ax_cols), BF),
            pltpu.VMEM((q_own, own_k, channels, 2 * channels), F32),
            dma(q_own),
        ],
        compiler_params=params(),
        name="input_gradient",
    )(pointwise_weight, grad_pre, flip(cos_low), flip(sin_low), cos_high, sin_high, gathered, spec, weight_grad)
    return (input_grad, spectral_grad, weight_grad)


def solution(mesh):
    field = P(None, "radial", ("parts", "axial"))
    return jax.shard_map(
        body,
        mesh=mesh,
        in_specs=(field, field, field, P(), P("radial", "axial", None, None)),
        out_specs=(field, P("radial", ("parts", "axial"), None, None), P("parts", None)),
        check_vma=False,
    )
```
